32 devices in a mesh: group: 1, expert: 16 (over z, y, x), seq: 2 (over core).
Axes of the slice: x: 2, y: 2, z: 4, core: 2. Of those that a mesh axis runs over, the one named last changes fastest.
Arguments:
- tokens: bfloat16 [2, 4096, 1664], P(('group', 'seq'), 'expert'), may hold values from -6 to 6
- router_w: bfloat16 [1664, 4], replicated, may hold values from -0.15625 to 0.15625
- expert_ids: int32 [2, 4096, 2], P(('group', 'seq'), 'expert'), may hold values from 0 to 3, all different within a row; in each aligned block of 256 rows (0 to 255, 256 to 511, ..., all dimensions but the last counted through in order) at most 256 rows name the same one
- w_in: bfloat16 [16, 1664, 2048], P('expert', None, 'seq'), may hold values from -0.15625 to 0.15625
- w_out: bfloat16 [16, 2048, 1664], P('expert', 'seq'), may hold values from -0.0625 to 0.0625
- w_qkv: bfloat16 [3, 1664, 832], P(None, None, 'seq'), may hold values from -0.15625 to 0.15625
Outputs:
- mixed: bfloat16 [2, 4096, 1664], P(('group', 'seq'), 'expert')
- attended: bfloat16 [2, 4096, 832], P('group', 'expert', 'seq')
The draws below stay inside these ranges and needn't reach their ends.
Inputs may be any that keep to these rules, and one draw needn't show every extreme that they name: `expert_ids`: in each aligned block of 256 tokens (the tokens of one device, images taken in order) no expert is named by more than 256 of the choices, and this bound is reached; the two experts of a token differ.
All inputs are finite; a program needn't handle non-finite values.
Results may differ from the reference program's by a relative error of at most 0.019.
Values may be sent and summed in bfloat16 or wider, within the bound.
A program may use at most 192 MiB of HBM per device.

```python
import math
import jax
import jax.numpy as jnp
import numpy as np
from jax import lax

D = 1664
FF = 8192
HD = 104
HEADS = 8
LEN = 4096
SPLIT = 4
IMAGES = 2
EXPERTS = 4
TOK_DEV = 256
MOST = 256
SLOT = 192


def level_of(own_key, extent, split, least, high):
    factor_of, own = 1.0, jax.random.fold_in(own_key, 6)
    for dim, blocks in split:
        heights = jnp.exp(jax.random.uniform(jax.random.fold_in(own, dim), (blocks,), jnp.float32, least / len(split), high / len(split)))
        factor_of = factor_of * jnp.repeat(heights, extent[dim] // blocks).reshape([-1 if axis == dim else 1 for axis in range(len(extent))])
    return factor_of


def shared_out(stream_key, own, number, rows, count, top, reach, slope):
    sequence = jax.random.permutation(stream_key, count)
    crowded, ordinary = shares(count, rows * top, reach, slope, True), shares(count, rows * top, reach, slope, False)
    places = jnp.arange(count)

    def named(sizes, turn):
        used = int((sizes > 0).sum())
        fixed = max(1, used // 4)
        moved = fixed + (places - fixed + turn * (used - fixed)) % max(1, count - fixed)
        return jnp.zeros((count,), jnp.int32).at[sequence[jnp.where(places < fixed, places, moved)]].set(jnp.asarray(sizes, jnp.int32))

    sizes = jnp.where(number % 4 == 0, named(crowded, number // 4), named(ordinary, number - number // 4 - 1))
    mixed = jax.random.permutation(jax.random.fold_in(own, 3), count)
    giver, taker = mixed[0:count // 2 * 2:2], mixed[1:count // 2 * 2:2]
    margin = jnp.minimum(sizes[giver] - 1, reach - sizes[taker]) // 2
    margin = jnp.where((giver == sequence[0]) | (taker == sequence[0]) | (sizes[taker] == 0), 0, jnp.maximum(margin, 0))
    moved = jax.random.randint(jax.random.fold_in(own, 4), (count // 2,), 0, 1 << 20) % (margin + 1)
    sizes = sizes.at[giver].add(-moved).at[taker].add(moved)
    labels = jnp.searchsorted(jnp.cumsum(sizes), jnp.arange(rows * top), side="right").astype(jnp.int32)
    listing = labels.reshape(top, rows).T
    listing = listing[jax.random.permutation(jax.random.fold_in(own, 1), rows)]
    turn = jax.random.randint(jax.random.fold_in(own, 2), (rows, 1), 0, top)
    return jnp.take_along_axis(listing, (jnp.arange(top)[None, :] + turn) % top, axis=1)


def shares(count, total, limit, skew, full):
    weights = [(1 << 20) // math.isqrt(grade ** skew) + 1 for grade in range(1, count + 1)]
    largest = limit if full else min(limit, max(-(-total // count), total * weights[0] // sum(weights)))
    least = 1 if total - largest >= count - 1 else 0
    holding, spare = [largest] + [least] * (count - 1), total - largest - least * (count - 1)
    while spare > 0:
        candidates = [i for i in range(1, count) if holding[i] < largest] or [i for i in range(1, count) if holding[i] < limit]
        pool, left = sum([weights[i] for i in candidates]), spare
        for i in candidates:
            extra = min(limit - holding[i], max(1, left * weights[i] // pool), spare)
            holding[i] = holding[i] + extra
            spare = spare - extra
    return np.array(holding)


def normal_values(key, extent, scale, most, pieces=(), kind=jnp.bfloat16):
    values = jax.random.normal(key, extent, jnp.float32) * scale
    if len(pieces) > 0:
        values = level_of(key, extent, pieces, -0.22, 0.18) * values
    return jnp.clip(values, min=-most, max=most).astype(kind)


def setup_inputs(seed: int = 0, part: int = 0) -> dict:
    arg_keys = jax.random.split(jax.random.key(seed), 7)
    own_keys = jax.random.split(jax.random.fold_in(arg_keys[6], part), 7)
    tokens = normal_values(own_keys[0], (IMAGES, LEN, D), 1.0, 6.0, ((0, 2), (1, 16)))
    router_w = normal_values(arg_keys[1], (D, EXPERTS), D ** -0.5, 0.15625)
    expert_ids_keys = jax.random.split(jax.random.fold_in(own_keys[2], 1), IMAGES * LEN // TOK_DEV)
    expert_ids_turns = jax.random.permutation(jax.random.fold_in(own_keys[2], 3), IMAGES * LEN // TOK_DEV)
    expert_ids = jax.vmap(lambda own, number: shared_out(jax.random.fold_in(own_keys[2], 2), own, number, TOK_DEV, EXPERTS, 2, MOST, 2))(expert_ids_keys, expert_ids_turns).reshape((IMAGES, LEN, 2))
    w_in = normal_values(arg_keys[3], (EXPERTS * SPLIT, D, FF // SPLIT), D ** -0.5, 0.15625, ((0, 16), (2, 2)))
    w_out = normal_values(arg_keys[4], (EXPERTS * SPLIT, FF // SPLIT, D), FF ** -0.5, 0.0625, ((0, 16), (1, 2)))
    w_qkv = normal_values(arg_keys[5], (3, D, HEADS * HD), D ** -0.5, 0.15625, ((2, 2),))
    return dict(tokens=tokens, router_w=router_w, expert_ids=expert_ids, w_in=w_in, w_out=w_out, w_qkv=w_qkv)


def layer_norm(values):
    values = values.astype(jnp.float32)
    center = lax.optimization_barrier(jnp.mean(values, axis=-1, keepdims=True))
    spread = lax.optimization_barrier(jnp.mean(jnp.square(values - center), axis=-1, keepdims=True))
    return ((values - center) * lax.rsqrt(spread + 1e-06)).astype(jnp.bfloat16)

def gate_pair(normed, flat_ids, router_w):
    logits = jnp.dot(normed, router_w, preferred_element_type=jnp.float32)
    chosen = jnp.take_along_axis(logits, flat_ids, axis=1)
    first = jax.nn.sigmoid(chosen[:, 0] - chosen[:, 1])
    second = jax.nn.sigmoid(chosen[:, 1] - chosen[:, 0])
    return (first, second)

def kept_choices(flat_ids):
    blocked = flat_ids.reshape(-1, TOK_DEV * 2)
    onehot = (blocked[:, :, None] == jnp.arange(EXPERTS, dtype=jnp.int32)[None, None, :]).astype(jnp.int32)
    before = jnp.cumsum(onehot, axis=1) - onehot
    position = lax.optimization_barrier(jnp.sum(before * onehot, axis=2))
    return (position < SLOT).astype(jnp.int32).reshape(-1, 2)

def expert_outputs(normed, flat_ids, kept, w_in, w_out):
    pair_ids = jnp.where(kept > 0, flat_ids, EXPERTS).reshape(-1).astype(jnp.int32)
    pair_count = pair_ids.shape[0]
    order = jnp.argsort(pair_ids, stable=True).astype(jnp.int32)
    sorted_ids = pair_ids[order]
    block_rows = min(256, pair_count)
    width = normed.shape[1]

    def one_block(block_index):
        picks = lax.dynamic_slice_in_dim(order, block_index * block_rows, block_rows)
        owners = lax.dynamic_slice_in_dim(sorted_ids, block_index * block_rows, block_rows)
        rows = normed[picks // 2]

        def one_expert(expert_index, totals):
            first_part = lax.dynamic_slice_in_dim(w_in, expert_index * SPLIT, SPLIT, 0)
            w_first = jnp.transpose(first_part, (1, 0, 2)).reshape(width, FF)
            w_second = lax.dynamic_slice_in_dim(w_out, expert_index * SPLIT, SPLIT, 0).reshape(FF, width)
            hidden = jax.nn.gelu(jnp.dot(rows, w_first, preferred_element_type=jnp.float32)).astype(jnp.bfloat16)
            result = jnp.dot(hidden, w_second, preferred_element_type=jnp.float32)
            return jnp.where((owners == expert_index)[:, None], result, totals)
        start_expert = owners[0].astype(jnp.int32)
        end_expert = jnp.minimum(owners[block_rows - 1] + 1, EXPERTS).astype(jnp.int32)
        return lax.fori_loop(start_expert, end_expert, one_expert, jnp.zeros((block_rows, width), jnp.float32))
    results = lax.map(one_block, jnp.arange(pair_count // block_rows, dtype=jnp.int32))
    placed = jnp.zeros((pair_count, width), jnp.float32).at[order].set(results.reshape(pair_count, width))
    return placed.reshape(-1, 2, width)

def attention(attn_in, w_qkv):
    count = attn_in.shape[0]
    proj = jnp.einsum('rd,cdf->crf', attn_in.astype(jnp.float32), w_qkv.astype(jnp.float32)).astype(jnp.bfloat16)
    heads = proj.shape[2] // HD
    per_head = jnp.transpose(proj.reshape(3, count, heads, HD), (2, 0, 1, 3))
    scale = 1.0 / math.sqrt(HD)

    def one_head(stack):
        scores = jnp.dot(stack[0], stack[1].T, preferred_element_type=jnp.float32) * scale
        weights = jnp.exp(scores)
        totals = lax.optimization_barrier(jnp.sum(weights, axis=1, keepdims=True))
        summed = jnp.dot(weights.astype(jnp.bfloat16), stack[2], preferred_element_type=jnp.float32)
        return (summed / totals).astype(jnp.bfloat16)
    results = lax.map(one_head, per_head)
    return jnp.transpose(results, (1, 0, 2)).reshape(count, heads * HD)

def reference(tokens, router_w, expert_ids, w_in, w_out, w_qkv):
    width = tokens.shape[2]
    flat_tokens = tokens.reshape(-1, width)
    flat_ids = expert_ids.reshape(-1, 2).astype(jnp.int32)
    normed = layer_norm(flat_tokens)
    first, second = gate_pair(normed, flat_ids, router_w)
    kept = kept_choices(flat_ids)
    pair_out = expert_outputs(normed, flat_ids, kept, w_in, w_out)
    keep_float = kept.astype(jnp.float32)
    combined = (first * keep_float[:, 0])[:, None] * pair_out[:, 0] + (second * keep_float[:, 1])[:, None] * pair_out[:, 1]
    mixed = (flat_tokens.astype(jnp.float32) + combined).astype(jnp.bfloat16).reshape(tokens.shape)
    attended = jnp.stack([attention(layer_norm(mixed[image]), w_qkv) for image in range(IMAGES)], axis=0)
    return (mixed, attended)
```

```python
import functools
import math

import jax
import jax.numpy as jnp
from jax import lax
from jax.experimental import pallas as pl
from jax.experimental.pallas import tpu as pltpu
from jax.sharding import PartitionSpec as P

HD = 104
SPLIT = 4
MIB = 1024 * 1024


def layer_norm(values):
    values = values.astype(jnp.float32)
    center = jnp.mean(values, axis=-1, keepdims=True)
    spread = jnp.mean(jnp.square(values - center), axis=-1, keepdims=True)
    return ((values - center) * lax.rsqrt(spread + 1e-06)).astype(jnp.bfloat16)


def gelu(value):
    inner = math.sqrt(2.0 / math.pi) * (value + 0.044715 * value * value * value)
    return 0.5 * value * (1.0 + jnp.tanh(inner))


def mlp_kernel(steps, chunk, has_base, rows_ref, *refs):
    w_in_refs, w_out_refs = refs[0:2], refs[2:4]
    base_ref = refs[4] if has_base else None
    out_ref, acc_ref = refs[-2], refs[-1]
    j = pl.program_id(0)
    count = rows_ref.shape[0]

    @pl.when(j == 0)
    def _():
        if has_base:
            acc_ref[...] = base_ref[...].astype(jnp.float32)
        else:
            acc_ref[...] = jnp.zeros_like(acc_ref)

    for block in range(2):

        @pl.when(j // steps == block)
        def _():
            for start in range(0, count, chunk):
                part = pl.ds(start, chunk)
                up = jnp.dot(
                    rows_ref[part, :], w_in_refs[block][...], preferred_element_type=jnp.float32
                )
                hidden = gelu(up).astype(jnp.bfloat16)
                acc_ref[part, :] += jnp.dot(
                    hidden, w_out_refs[block][...], preferred_element_type=jnp.float32
                )

    @pl.when(j == 2 * steps - 1)
    def _():
        out_ref[...] = acc_ref[...].astype(out_ref.dtype)


def mlp(rows, w_ins, w_outs, base, out_dtype):
    count, width = rows.shape
    units = w_ins[0].shape[1]
    tile = 512 if units % 512 == 0 else units
    steps = units // tile
    chunk = 256 if count % 256 == 0 else count

    def in_map(block):
        return lambda j: (0, jnp.clip(j - block * steps, 0, steps - 1))

    def out_map(block):
        return lambda j: (jnp.clip(j - block * steps, 0, steps - 1), 0)

    whole = pl.BlockSpec((count, width), lambda j: (0, 0))
    in_specs = [whole]
    in_specs += [pl.BlockSpec((width, tile), in_map(b)) for b in range(2)]
    in_specs += [pl.BlockSpec((tile, width), out_map(b)) for b in range(2)]
    operands = [rows, *w_ins, *w_outs]
    if base is not None:
        in_specs.append(whole)
        operands.append(base)
    return pl.pallas_call(
        functools.partial(mlp_kernel, steps, chunk, base is not None),
        grid=(2 * steps,),
        out_shape=jax.ShapeDtypeStruct((count, width), out_dtype),
        in_specs=in_specs,
        out_specs=whole,
        scratch_shapes=[pltpu.VMEM((count, width), jnp.float32)],
        compiler_params=pltpu.CompilerParams(
            vmem_limit_bytes=56 * MIB, dimension_semantics=("arbitrary",)
        ),
        cost_estimate=pl.CostEstimate(
            flops=8 * count * width * units,
            bytes_accessed=8 * width * units + 10 * count * width,
            transcendentals=2 * count * units,
        ),
    )(*operands)


def attention_kernel(key_tile, q_ref, k_ref, v_ref, out_ref):
    queries = q_ref[...]
    factor = math.log2(math.e) / math.sqrt(HD)
    width = queries.shape[1]
    total = jnp.zeros((1, width), jnp.float32)
    summed = jnp.zeros((HD, width), jnp.float32)
    for start in range(0, k_ref.shape[0], key_tile):
        part = pl.ds(start, key_tile)
        scores = jnp.dot(k_ref[part, :], queries, preferred_element_type=jnp.float32)
        weights = jnp.exp2(scores * factor)
        total += jnp.sum(weights, axis=0, keepdims=True)
        summed += jnp.dot(
            v_ref[:, part], weights.astype(jnp.bfloat16), preferred_element_type=jnp.float32
        )
    out_ref[...] = (summed / total).astype(out_ref.dtype)


def attention(queries, keys, values):
    columns = queries.shape[1]
    key_count = keys.shape[0]
    tile = 512 if columns % 512 == 0 else columns
    key_tile = 512 if key_count % 512 == 0 else key_count
    return pl.pallas_call(
        functools.partial(attention_kernel, key_tile),
        grid=(columns // tile,),
        out_shape=jax.ShapeDtypeStruct((HD, columns), jnp.bfloat16),
        in_specs=[
            pl.BlockSpec((HD, tile), lambda j: (0, j)),
            pl.BlockSpec((key_count, HD), lambda j: (0, 0)),
            pl.BlockSpec((HD, key_count), lambda j: (0, 0)),
        ],
        out_specs=pl.BlockSpec((HD, tile), lambda j: (0, j)),
        compiler_params=pltpu.CompilerParams(
            vmem_limit_bytes=48 * MIB, dimension_semantics=("arbitrary",)
        ),
        cost_estimate=pl.CostEstimate(
            flops=4 * HD * columns * key_count,
            bytes_accessed=4 * HD * (columns + key_count),
            transcendentals=columns * key_count,
        ),
    )(queries, keys, values)


def shards(places, tokens, router_w, expert_ids, w_in, w_out, w_qkv):
    row_count = tokens.shape[1]
    width = tokens.shape[2]
    experts = router_w.shape[1]
    slots = max(2, 3 * row_count // experts)
    columns = [[e * SPLIT + q for e in range(experts)] for q in range(SPLIT)]

    def across(value, bit):
        return lax.ppermute(value, "expert", [(p, p ^ bit) for p in range(places)])

    def other_core(value):
        return lax.ppermute(value, "seq", [(0, 1), (1, 0)])

    own_weights = (w_in[0], w_out[0])
    core_weights = tuple(other_core(w) for w in own_weights)
    far_weights = tuple(across(w, 1) for w in own_weights)
    far_core_weights = tuple(other_core(w) for w in far_weights)

    own_tokens = tokens[0]
    own_ids = expert_ids[0]
    normed = layer_norm(own_tokens)
    logits = jnp.dot(normed, router_w, preferred_element_type=jnp.float32)
    expert_range = jnp.arange(experts, dtype=jnp.int32)
    first_pick = jnp.sum(jnp.where(own_ids[:, 0:1] == expert_range[None, :], logits, 0.0), axis=1)
    second_pick = jnp.sum(jnp.where(own_ids[:, 1:2] == expert_range[None, :], logits, 0.0), axis=1)
    first_gate = jax.nn.sigmoid(first_pick - second_pick)
    second_gate = jax.nn.sigmoid(second_pick - first_pick)
    pair_ids = own_ids.reshape(row_count * 2)
    onehot = (pair_ids[:, None] == expert_range[None, :]).astype(jnp.int32)
    before = jnp.cumsum(onehot, axis=0) - onehot
    position = jnp.sum(before * onehot, axis=1)
    slot_index = jnp.where(position < slots, pair_ids * slots + position, -1)
    slot_index = slot_index.reshape(row_count, 2)
    slot_range = jnp.arange(experts * slots, dtype=jnp.int32)
    is_first = slot_index[:, 0:1] == slot_range[None, :]
    is_second = slot_index[:, 1:2] == slot_range[None, :]
    select = (is_first | is_second).astype(jnp.bfloat16)
    packed = lax.dot_general(
        select, normed, (((0,), (0,)), ((), ())), preferred_element_type=jnp.float32
    ).astype(jnp.bfloat16)
    outgoing = packed.reshape(experts, slots, width)
    received = lax.all_to_all(
        outgoing, "expert", split_axis=0, concat_axis=0, tiled=True, axis_index_groups=columns
    )
    near_rows = received.reshape(experts * slots, width)
    far_rows = across(near_rows, 2)

    chip_in, chip_out = zip(own_weights, core_weights)
    next_in, next_out = zip(far_weights, far_core_weights)
    near_sum = mlp(near_rows, chip_in, chip_out, None, jnp.float32)
    far_sum = mlp(far_rows, chip_in, chip_out, None, jnp.float32)
    far_sum = mlp(far_rows, next_in, next_out, far_sum, jnp.bfloat16)
    arrived = across(far_sum, 2)
    near_sum = mlp(near_rows, next_in, next_out, near_sum, jnp.float32)
    summed = (near_sum + arrived.astype(jnp.float32)).astype(jnp.bfloat16)
    merged = lax.all_to_all(
        summed.reshape(experts, slots, width),
        "expert",
        split_axis=0,
        concat_axis=0,
        tiled=True,
        axis_index_groups=columns,
    ).reshape(experts * slots, width)

    gates = jnp.where(is_first, first_gate[:, None], 0.0) + jnp.where(
        is_second, second_gate[:, None], 0.0
    )
    high = gates.astype(jnp.bfloat16)
    low = (gates - high.astype(jnp.float32)).astype(jnp.bfloat16)
    combined = jnp.dot(high, merged, preferred_element_type=jnp.float32) + jnp.dot(
        low, merged, preferred_element_type=jnp.float32
    )
    mixed = (own_tokens.astype(jnp.float32) + combined).astype(jnp.bfloat16)
    attn_local = layer_norm(mixed)
    attn_in = lax.all_gather(attn_local[None], "seq", axis=0, tiled=True)
    images = attn_in.shape[0]
    proj = jnp.einsum("cdf,ird->cifr", w_qkv, attn_in, preferred_element_type=jnp.float32).astype(
        jnp.bfloat16
    )
    heads = proj.shape[2] // HD
    pairs = images * heads
    share = places // pairs
    part = row_count // share
    proj = proj.reshape(3, pairs, HD, row_count)
    query_parts = proj[0].reshape(pairs, HD, share, part).transpose(0, 2, 1, 3)
    key_parts = jnp.broadcast_to(proj[1][:, None], (pairs, share, HD, row_count))
    value_parts = jnp.broadcast_to(proj[2][:, None], (pairs, share, HD, row_count))
    leaving = jnp.concatenate([key_parts, value_parts, query_parts], axis=3).reshape(
        places, HD, 2 * row_count + part
    )
    landed = lax.all_to_all(leaving, "expert", split_axis=0, concat_axis=0, tiled=True)
    keys = landed[:, :, :row_count].transpose(0, 2, 1).reshape(places * row_count, HD)
    values = landed[:, :, row_count : 2 * row_count].transpose(1, 0, 2)
    values = values.reshape(HD, places * row_count)
    queries = landed[:, :, 2 * row_count :].transpose(1, 0, 2).reshape(HD, places * part)
    result = attention(queries, keys, values)
    result = result.reshape(HD, places, part).transpose(1, 0, 2)
    returned = lax.all_to_all(result, "expert", split_axis=0, concat_axis=0, tiled=True)
    attended = returned.reshape(images, heads, share, HD, part).transpose(0, 2, 4, 1, 3)
    attended = attended.reshape(images, row_count, heads * HD)
    return (mixed[None], attended)


def solution(mesh):
    in_specs = (
        P(("group", "seq"), "expert", None),
        P(),
        P(("group", "seq"), "expert", None),
        P("expert", None, "seq"),
        P("expert", "seq", None),
        P(None, None, "seq"),
    )
    out_specs = (P(("group", "seq"), "expert", None), P("group", "expert", "seq"))
    return jax.shard_map(
        functools.partial(shards, mesh.shape["expert"]),
        mesh=mesh,
        in_specs=in_specs,
        out_specs=out_specs,
        check_vma=False,
    )
```

```python
import functools
import math

import jax
import jax.numpy as jnp
from jax import lax
from jax.experimental import pallas as pl
from jax.experimental.pallas import tpu as pltpu
from jax.sharding import PartitionSpec as P

HD = 104
SPLIT = 4
MIB = 1024 * 1024


def layer_norm(values):
    values = values.astype(jnp.float32)
    center = jnp.mean(values, axis=-1, keepdims=True)
    spread = jnp.mean(jnp.square(values - center), axis=-1, keepdims=True)
    return ((values - center) * lax.rsqrt(spread + 1e-06)).astype(jnp.bfloat16)


def gelu(value):
    inner = math.sqrt(2.0 / math.pi) * (value + 0.044715 * value * value * value)
    return 0.5 * value * (1.0 + jnp.tanh(inner))


def mlp_kernel(steps, parts, has_base, *refs):
    rows_refs, refs = refs[:parts], refs[parts:]
    w_in_refs, w_out_refs, refs = refs[0:2], refs[2:4], refs[4:]
    base_refs = refs[:parts] if has_base else None
    out_refs, acc_refs = refs[-2 * parts : -parts], refs[-parts:]
    j = pl.program_id(0)

    @pl.when(j == 0)
    def _():
        for p in range(parts):
            if has_base:
                acc_refs[p][...] = base_refs[p][...].astype(jnp.float32)
            else:
                acc_refs[p][...] = jnp.zeros_like(acc_refs[p])

    for block in range(2):

        @pl.when(j // steps == block)
        def _():
            for p in range(parts):
                up = jnp.dot(
                    rows_refs[p][...], w_in_refs[block][...], preferred_element_type=jnp.float32
                )
                hidden = gelu(up).astype(jnp.bfloat16)
                acc_refs[p][...] += jnp.dot(
                    hidden, w_out_refs[block][...], preferred_element_type=jnp.float32
                )

    @pl.when(j == 2 * steps - 1)
    def _():
        for p in range(parts):
            out_refs[p][...] = acc_refs[p][...].astype(out_refs[p].dtype)


def mlp(rows, w_ins, w_outs, base, out_dtype, most=512):
    parts = len(rows)
    count, width = rows[0].shape
    units = w_ins[0].shape[1]
    tile = most if units % most == 0 else units
    steps = units // tile

    def in_map(block):
        return lambda j: (0, jnp.clip(j - block * steps, 0, steps - 1))

    def out_map(block):
        return lambda j: (jnp.clip(j - block * steps, 0, steps - 1), 0)

    whole = pl.BlockSpec((count, width), lambda j: (0, 0))
    in_specs = [whole] * parts
    in_specs += [pl.BlockSpec((width, tile), in_map(b)) for b in range(2)]
    in_specs += [pl.BlockSpec((tile, width), out_map(b)) for b in range(2)]
    operands = [*rows, *w_ins, *w_outs]
    if base is not None:
        in_specs += [whole] * parts
        operands += [*base]
    return pl.pallas_call(
        functools.partial(mlp_kernel, steps, parts, base is not None),
        grid=(2 * steps,),
        out_shape=[jax.ShapeDtypeStruct((count, width), out_dtype)] * parts,
        in_specs=in_specs,
        out_specs=[whole] * parts,
        scratch_shapes=[pltpu.VMEM((count, width), jnp.float32)] * parts,
        compiler_params=pltpu.CompilerParams(
            vmem_limit_bytes=60 * MIB, dimension_semantics=("arbitrary",)
        ),
        cost_estimate=pl.CostEstimate(
            flops=8 * parts * count * width * units,
            bytes_accessed=8 * width * units + 10 * parts * count * width,
            transcendentals=2 * parts * count * units,
        ),
    )(*operands)


def attention_kernel(key_tile, q_ref, k_ref, v_ref, out_ref):
    queries = q_ref[...]
    factor = math.log2(math.e) / math.sqrt(HD)
    width = queries.shape[1]
    total = jnp.zeros((1, width), jnp.float32)
    summed = jnp.zeros((HD, width), jnp.float32)
    for start in range(0, k_ref.shape[0], key_tile):
        part = pl.ds(start, key_tile)
        scores = jnp.dot(k_ref[part, :], queries, preferred_element_type=jnp.float32)
        weights = jnp.exp2(scores * factor)
        total += jnp.sum(weights, axis=0, keepdims=True)
        summed += jnp.dot(
            v_ref[:, part], weights.astype(jnp.bfloat16), preferred_element_type=jnp.float32
        )
    out_ref[...] = (summed / total).astype(out_ref.dtype)


def attention(queries, keys, values):
    columns = queries.shape[1]
    key_count = keys.shape[0]
    tile = 512 if columns % 512 == 0 else columns
    key_tile = 512 if key_count % 512 == 0 else key_count
    return pl.pallas_call(
        functools.partial(attention_kernel, key_tile),
        grid=(columns // tile,),
        out_shape=jax.ShapeDtypeStruct((HD, columns), jnp.bfloat16),
        in_specs=[
            pl.BlockSpec((HD, tile), lambda j: (0, j)),
            pl.BlockSpec((key_count, HD), lambda j: (0, 0)),
            pl.BlockSpec((HD, key_count), lambda j: (0, 0)),
        ],
        out_specs=pl.BlockSpec((HD, tile), lambda j: (0, j)),
        compiler_params=pltpu.CompilerParams(
            vmem_limit_bytes=48 * MIB, dimension_semantics=("arbitrary",)
        ),
        cost_estimate=pl.CostEstimate(
            flops=4 * HD * columns * key_count,
            bytes_accessed=4 * HD * (columns + key_count),
            transcendentals=columns * key_count,
        ),
    )(queries, keys, values)


def shards(places, tokens, router_w, expert_ids, w_in, w_out, w_qkv):
    row_count = tokens.shape[1]
    width = tokens.shape[2]
    experts = router_w.shape[1]
    slots = max(2, 3 * row_count // experts)
    columns = [[e * SPLIT + q for e in range(experts)] for q in range(SPLIT)]

    def across(value, bit):
        return lax.ppermute(value, "expert", [(p, p ^ bit) for p in range(places)])

    def other_core(value):
        return lax.ppermute(value, "seq", [(0, 1), (1, 0)])

    own_weights = (w_in[0], w_out[0])
    far_weights = tuple(across(w, 1) for w in own_weights)
    core_weights = tuple(other_core(w) for w in own_weights)

    own_tokens = tokens[0]
    own_ids = expert_ids[0]
    normed = layer_norm(own_tokens)
    logits = jnp.dot(normed, router_w, preferred_element_type=jnp.float32)
    expert_range = jnp.arange(experts, dtype=jnp.int32)
    first_pick = jnp.sum(jnp.where(own_ids[:, 0:1] == expert_range[None, :], logits, 0.0), axis=1)
    second_pick = jnp.sum(jnp.where(own_ids[:, 1:2] == expert_range[None, :], logits, 0.0), axis=1)
    first_gate = jax.nn.sigmoid(first_pick - second_pick)
    second_gate = jax.nn.sigmoid(second_pick - first_pick)
    pair_ids = own_ids.reshape(row_count * 2)
    onehot = (pair_ids[:, None] == expert_range[None, :]).astype(jnp.int32)
    before = jnp.cumsum(onehot, axis=0) - onehot
    position = jnp.sum(before * onehot, axis=1)
    slot_index = jnp.where(position < slots, pair_ids * slots + position, -1)
    slot_index = slot_index.reshape(row_count, 2)
    parts = 2 if slots % 2 == 0 else 1
    part_slots = slots // parts
    slot_range = (
        jnp.arange(experts, dtype=jnp.int32)[:, None] * slots
        + jnp.arange(part_slots, dtype=jnp.int32)[None, :]
    ).reshape(1, experts * part_slots)

    def between_planes(value):
        return lax.all_to_all(
            value.reshape(experts, part_slots, width),
            "expert",
            split_axis=0,
            concat_axis=0,
            tiled=True,
            axis_index_groups=columns,
        ).reshape(experts * part_slots, width)

    near_rows, far_rows, gate_parts = [], [], []
    for p in range(parts):
        is_first = slot_index[:, 0:1] == slot_range + p * part_slots
        is_second = slot_index[:, 1:2] == slot_range + p * part_slots
        select = (is_first | is_second).astype(jnp.bfloat16)
        packed = lax.dot_general(
            select, normed, (((0,), (0,)), ((), ())), preferred_element_type=jnp.float32
        ).astype(jnp.bfloat16)
        near_rows.append(between_planes(packed))
        far_rows.append(across(near_rows[p], 2))
        gates = jnp.where(is_first, first_gate[:, None], 0.0) + jnp.where(
            is_second, second_gate[:, None], 0.0
        )
        high = gates.astype(jnp.bfloat16)
        gate_parts.append((high, (gates - high.astype(jnp.float32)).astype(jnp.bfloat16)))

    chip_in, chip_out = zip(own_weights, core_weights)
    near_sum = mlp(near_rows, chip_in, chip_out, None, jnp.float32)
    far_sum = mlp(far_rows, chip_in, chip_out, None, jnp.float32)
    far_weights, near_sum, far_sum = lax.optimization_barrier((far_weights, near_sum, far_sum))
    far_core_weights = tuple(other_core(w) for w in far_weights)
    next_in, next_out = zip(far_weights, far_core_weights)
    sent = []
    for p in range(parts):
        sent += mlp(far_rows[p : p + 1], next_in, next_out, far_sum[p : p + 1], jnp.bfloat16)
        if p + 1 < parts:
            sent[p], far_sum = lax.optimization_barrier((sent[p], far_sum))
    arrived = [across(value, 2) for value in sent]
    near_sum = mlp(near_rows, next_in, next_out, near_sum, jnp.float32)
    combined = own_tokens.astype(jnp.float32)
    for p in range(parts):
        summed = (near_sum[p] + arrived[p].astype(jnp.float32)).astype(jnp.bfloat16)
        merged = between_planes(summed)
        for gate in gate_parts[p]:
            combined += jnp.dot(gate, merged, preferred_element_type=jnp.float32)
    mixed = combined.astype(jnp.bfloat16)
    attn_local = layer_norm(mixed)
    attn_other = other_core(attn_local)
    own_proj, other_proj = [
        jnp.einsum("cdf,rd->cfr", w_qkv, value, preferred_element_type=jnp.float32).astype(
            jnp.bfloat16
        )
        for value in (attn_local, attn_other)
    ]
    images = 2
    is_low = lax.axis_index("seq") == 0
    proj = jnp.stack(
        [jnp.where(is_low, own_proj, other_proj), jnp.where(is_low, other_proj, own_proj)], axis=1
    )
    heads = proj.shape[2] // HD
    pairs = images * heads
    share = places // pairs
    part = row_count // share
    proj = proj.reshape(3, pairs, HD, row_count)
    query_parts = proj[0].reshape(pairs, HD, share, part).transpose(0, 2, 1, 3)
    key_parts = jnp.broadcast_to(proj[1][:, None], (pairs, share, HD, row_count))
    value_parts = jnp.broadcast_to(proj[2][:, None], (pairs, share, HD, row_count))
    leaving = jnp.concatenate([key_parts, value_parts, query_parts], axis=3).reshape(
        places, HD, 2 * row_count + part
    )
    landed = lax.all_to_all(leaving, "expert", split_axis=0, concat_axis=0, tiled=True)
    keys = landed[:, :, :row_count].transpose(0, 2, 1).reshape(places * row_count, HD)
    values = landed[:, :, row_count : 2 * row_count].transpose(1, 0, 2)
    values = values.reshape(HD, places * row_count)
    queries = landed[:, :, 2 * row_count :].transpose(1, 0, 2).reshape(HD, places * part)
    result = attention(queries, keys, values)
    result = result.reshape(HD, places, part).transpose(1, 0, 2)
    returned = lax.all_to_all(result, "expert", split_axis=0, concat_axis=0, tiled=True)
    attended = returned.reshape(images, heads, share, HD, part).transpose(0, 2, 4, 1, 3)
    attended = attended.reshape(images, row_count, heads * HD)
    return (mixed[None], attended)


def solution(mesh):
    in_specs = (
        P(("group", "seq"), "expert", None),
        P(),
        P(("group", "seq"), "expert", None),
        P("expert", None, "seq"),
        P("expert", "seq", None),
        P(None, None, "seq"),
    )
    out_specs = (P(("group", "seq"), "expert", None), P("group", "expert", "seq"))
    return jax.shard_map(
        functools.partial(shards, mesh.shape["expert"]),
        mesh=mesh,
        in_specs=in_specs,
        out_specs=out_specs,
        check_vma=False,
    )
```

```python
import functools
import math

import jax
import jax.numpy as jnp
from jax import lax
from jax.experimental import pallas as pl
from jax.experimental.pallas import tpu as pltpu
from jax.sharding import PartitionSpec as P

HD = 104
SPLIT = 4
MIB = 1024 * 1024


def layer_norm(values):
    values = values.astype(jnp.float32)
    center = jnp.mean(values, axis=-1, keepdims=True)
    spread = jnp.mean(jnp.square(values - center), axis=-1, keepdims=True)
    return ((values - center) * lax.rsqrt(spread + 1e-06)).astype(jnp.bfloat16)


def gelu(value):
    inner = math.sqrt(2.0 / math.pi) * (value + 0.044715 * value * value * value)
    return 0.5 * value * (1.0 + jnp.tanh(inner))


def mlp_kernel(steps, parts, has_base, *refs):
    rows_refs, refs = refs[:parts], refs[parts:]
    w_in_refs, w_out_refs, refs = refs[0:2], refs[2:4], refs[4:]
    base_refs = refs[:parts] if has_base else None
    out_refs, acc_refs = refs[-2 * parts : -parts], refs[-parts:]
    j = pl.program_id(0)

    @pl.when(j == 0)
    def _():
        for p in range(parts):
            if has_base:
                acc_refs[p][...] = base_refs[p][...].astype(jnp.float32)
            else:
                acc_refs[p][...] = jnp.zeros_like(acc_refs[p])

    for block in range(2):

        @pl.when(j // steps == block)
        def _():
            for p in range(parts):
                up = jnp.dot(
                    rows_refs[p][...], w_in_refs[block][...], preferred_element_type=jnp.float32
                )
                hidden = gelu(up).astype(jnp.bfloat16)
                acc_refs[p][...] += jnp.dot(
                    hidden, w_out_refs[block][...], preferred_element_type=jnp.float32
                )

    @pl.when(j == 2 * steps - 1)
    def _():
        for p in range(parts):
            out_refs[p][...] = acc_refs[p][...].astype(out_refs[p].dtype)


def mlp(rows, w_ins, w_outs, base, out_dtype, most=512):
    parts = len(rows)
    count, width = rows[0].shape
    units = w_ins[0].shape[1]
    tile = most if units % most == 0 else units
    steps = units // tile

    def in_map(block):
        return lambda j: (0, jnp.clip(j - block * steps, 0, steps - 1))

    def out_map(block):
        return lambda j: (jnp.clip(j - block * steps, 0, steps - 1), 0)

    whole = pl.BlockSpec((count, width), lambda j: (0, 0))
    in_specs = [whole] * parts
    in_specs += [pl.BlockSpec((width, tile), in_map(b)) for b in range(2)]
    in_specs += [pl.BlockSpec((tile, width), out_map(b)) for b in range(2)]
    operands = [*rows, *w_ins, *w_outs]
    if base is not None:
        in_specs += [whole] * parts
        operands += [*base]
    return pl.pallas_call(
        functools.partial(mlp_kernel, steps, parts, base is not None),
        grid=(2 * steps,),
        out_shape=[jax.ShapeDtypeStruct((count, width), out_dtype)] * parts,
        in_specs=in_specs,
        out_specs=[whole] * parts,
        scratch_shapes=[pltpu.VMEM((count, width), jnp.float32)] * parts,
        compiler_params=pltpu.CompilerParams(
            vmem_limit_bytes=60 * MIB, dimension_semantics=("arbitrary",)
        ),
        cost_estimate=pl.CostEstimate(
            flops=8 * parts * count * width * units,
            bytes_accessed=8 * width * units + 10 * parts * count * width,
            transcendentals=2 * parts * count * units,
        ),
    )(*operands)


def attention_kernel(key_tile, q_ref, k_ref, v_ref, out_ref):
    queries = q_ref[...]
    factor = math.log2(math.e) / math.sqrt(HD)
    width = queries.shape[1]
    total = jnp.zeros((1, width), jnp.float32)
    summed = jnp.zeros((HD, width), jnp.float32)
    for start in range(0, k_ref.shape[0], key_tile):
        part = pl.ds(start, key_tile)
        scores = jnp.dot(k_ref[part, :], queries, preferred_element_type=jnp.float32)
        weights = jnp.exp2(scores * factor)
        total += jnp.sum(weights, axis=0, keepdims=True)
        summed += jnp.dot(
            v_ref[:, part], weights.astype(jnp.bfloat16), preferred_element_type=jnp.float32
        )
    out_ref[...] = (summed / total).astype(out_ref.dtype)


def attention(queries, keys, values):
    columns = queries.shape[1]
    key_count = keys.shape[0]
    tile = 512 if columns % 512 == 0 else columns
    key_tile = 512 if key_count % 512 == 0 else key_count
    return pl.pallas_call(
        functools.partial(attention_kernel, key_tile),
        grid=(columns // tile,),
        out_shape=jax.ShapeDtypeStruct((HD, columns), jnp.bfloat16),
        in_specs=[
            pl.BlockSpec((HD, tile), lambda j: (0, j)),
            pl.BlockSpec((key_count, HD), lambda j: (0, 0)),
            pl.BlockSpec((HD, key_count), lambda j: (0, 0)),
        ],
        out_specs=pl.BlockSpec((HD, tile), lambda j: (0, j)),
        compiler_params=pltpu.CompilerParams(
            vmem_limit_bytes=48 * MIB, dimension_semantics=("arbitrary",)
        ),
        cost_estimate=pl.CostEstimate(
            flops=4 * HD * columns * key_count,
            bytes_accessed=4 * HD * (columns + key_count),
            transcendentals=columns * key_count,
        ),
    )(queries, keys, values)


def shards(places, tokens, router_w, expert_ids, w_in, w_out, w_qkv):
    row_count = tokens.shape[1]
    width = tokens.shape[2]
    experts = router_w.shape[1]
    slots = max(2, 3 * row_count // experts)
    columns = [[e * SPLIT + q for e in range(experts)] for q in range(SPLIT)]

    def across(value, bit):
        return lax.ppermute(value, "expert", [(p, p ^ bit) for p in range(places)])

    def other_core(value):
        return lax.ppermute(value, "seq", [(0, 1), (1, 0)])

    own_weights = (w_in[0], w_out[0])
    far_weights = tuple(across(w, 1) for w in own_weights)
    core_weights = tuple(other_core(w) for w in own_weights)

    own_tokens = tokens[0]
    own_ids = expert_ids[0]
    normed = layer_norm(own_tokens)
    logits = jnp.dot(normed, router_w, preferred_element_type=jnp.float32)
    expert_range = jnp.arange(experts, dtype=jnp.int32)
    first_pick = jnp.sum(jnp.where(own_ids[:, 0:1] == expert_range[None, :], logits, 0.0), axis=1)
    second_pick = jnp.sum(jnp.where(own_ids[:, 1:2] == expert_range[None, :], logits, 0.0), axis=1)
    first_gate = jax.nn.sigmoid(first_pick - second_pick)
    second_gate = jax.nn.sigmoid(second_pick - first_pick)
    pair_ids = own_ids.reshape(row_count * 2)
    onehot = (pair_ids[:, None] == expert_range[None, :]).astype(jnp.int32)
    before = jnp.cumsum(onehot, axis=0) - onehot
    position = jnp.sum(before * onehot, axis=1)
    slot_index = jnp.where(position < slots, pair_ids * slots + position, -1)
    slot_index = slot_index.reshape(row_count, 2)
    parts = 2 if slots % 2 == 0 else 1
    part_slots = slots // parts
    slot_range = (
        jnp.arange(experts, dtype=jnp.int32)[:, None] * slots
        + jnp.arange(part_slots, dtype=jnp.int32)[None, :]
    ).reshape(1, experts * part_slots)

    def between_planes(value):
        return lax.all_to_all(
            value.reshape(experts, -1, width),
            "expert",
            split_axis=0,
            concat_axis=0,
            tiled=True,
            axis_index_groups=columns,
        )

    packed, gate_parts = [], []
    for p in range(parts):
        is_first = slot_index[:, 0:1] == slot_range + p * part_slots
        is_second = slot_index[:, 1:2] == slot_range + p * part_slots
        select = (is_first | is_second).astype(jnp.bfloat16)
        rows = lax.dot_general(
            select, normed, (((0,), (0,)), ((), ())), preferred_element_type=jnp.float32
        ).astype(jnp.bfloat16)
        packed.append(rows.reshape(experts, part_slots, width))
        gates = jnp.where(is_first, first_gate[:, None], 0.0) + jnp.where(
            is_second, second_gate[:, None], 0.0
        )
        high = gates.astype(jnp.bfloat16)
        gate_parts.append((high, (gates - high.astype(jnp.float32)).astype(jnp.bfloat16)))

    received = between_planes(jnp.concatenate(packed, axis=1))
    near_rows = [
        received[:, p * part_slots : (p + 1) * part_slots].reshape(experts * part_slots, width)
        for p in range(parts)
    ]
    far_rows = [across(value, 2) for value in near_rows]
    chip_in, chip_out = zip(own_weights, core_weights)
    near_sum = mlp(near_rows, chip_in, chip_out, None, jnp.float32)
    far_sum = mlp(far_rows, chip_in, chip_out, None, jnp.float32)
    far_in, near_sum, far_sum = lax.optimization_barrier((far_weights[0], near_sum, far_sum))
    far_core_in = other_core(far_in)
    far_out, far_sum = lax.optimization_barrier((far_weights[1], far_sum))
    far_weights = (far_in, far_out)
    far_core_weights = (far_core_in, other_core(far_out))
    next_in, next_out = zip(far_weights, far_core_weights)
    sent = []
    for p in range(parts):
        sent += mlp(far_rows[p : p + 1], next_in, next_out, far_sum[p : p + 1], jnp.bfloat16)
        if p + 1 < parts:
            sent[p], far_sum = lax.optimization_barrier((sent[p], far_sum))
    arrived = [across(value, 2) for value in sent]
    near_sum, sent[-1] = lax.optimization_barrier((near_sum, sent[-1]))
    near_sum = [
        mlp(near_rows[p : p + 1], next_in, next_out, near_sum[p : p + 1], jnp.float32)[0]
        for p in range(parts)
    ]
    combined = own_tokens.astype(jnp.float32)
    for p in range(parts):
        summed = (near_sum[p] + arrived[p].astype(jnp.float32)).astype(jnp.bfloat16)
        merged = between_planes(summed).reshape(experts * part_slots, width)
        for gate in gate_parts[p]:
            combined += jnp.dot(gate, merged, preferred_element_type=jnp.float32)
    mixed = combined.astype(jnp.bfloat16)
    attn_local = layer_norm(mixed)
    attn_other = other_core(attn_local)
    own_proj, other_proj = [
        jnp.einsum("cdf,rd->cfr", w_qkv, value, preferred_element_type=jnp.float32).astype(
            jnp.bfloat16
        )
        for value in (attn_local, attn_other)
    ]
    images = 2
    is_low = lax.axis_index("seq") == 0
    proj = jnp.stack(
        [jnp.where(is_low, own_proj, other_proj), jnp.where(is_low, other_proj, own_proj)], axis=1
    )
    heads = proj.shape[2] // HD
    pairs = images * heads
    share = places // pairs
    part = row_count // share
    proj = proj.reshape(3, pairs, HD, row_count)
    query_parts = proj[0].reshape(pairs, HD, share, part).transpose(0, 2, 1, 3)
    key_parts = jnp.broadcast_to(proj[1][:, None], (pairs, share, HD, row_count))
    value_parts = jnp.broadcast_to(proj[2][:, None], (pairs, share, HD, row_count))
    leaving = jnp.concatenate([key_parts, value_parts, query_parts], axis=3).reshape(
        places, HD, 2 * row_count + part
    )
    landed = lax.all_to_all(leaving, "expert", split_axis=0, concat_axis=0, tiled=True)
    keys = landed[:, :, :row_count].transpose(0, 2, 1).reshape(places * row_count, HD)
    values = landed[:, :, row_count : 2 * row_count].transpose(1, 0, 2)
    values = values.reshape(HD, places * row_count)
    queries = landed[:, :, 2 * row_count :].transpose(1, 0, 2).reshape(HD, places * part)
    result = attention(queries, keys, values)
    result = result.reshape(HD, places, part).transpose(1, 0, 2)
    returned = lax.all_to_all(result, "expert", split_axis=0, concat_axis=0, tiled=True)
    attended = returned.reshape(images, heads, share, HD, part).transpose(0, 2, 4, 1, 3)
    attended = attended.reshape(images, row_count, heads * HD)
    return (mixed[None], attended)


def solution(mesh):
    in_specs = (
        P(("group", "seq"), "expert", None),
        P(),
        P(("group", "seq"), "expert", None),
        P("expert", None, "seq"),
        P("expert", "seq", None),
        P(None, None, "seq"),
    )
    out_specs = (P(("group", "seq"), "expert", None), P("group", "expert", "seq"))
    return jax.shard_map(
        functools.partial(shards, mesh.shape["expert"]),
        mesh=mesh,
        in_specs=in_specs,
        out_specs=out_specs,
        check_vma=False,
    )
```

```python
import functools
import math

import jax
import jax.numpy as jnp
from jax import lax
from jax.experimental import pallas as pl
from jax.experimental.pallas import tpu as pltpu
from jax.sharding import PartitionSpec as P

HD = 104
SPLIT = 4
MIB = 1024 * 1024


def layer_norm(values):
    values = values.astype(jnp.float32)
    center = jnp.mean(values, axis=-1, keepdims=True)
    spread = jnp.mean(jnp.square(values - center), axis=-1, keepdims=True)
    return ((values - center) * lax.rsqrt(spread + 1e-06)).astype(jnp.bfloat16)


def gelu(value):
    inner = math.sqrt(2.0 / math.pi) * (value + 0.044715 * value * value * value)
    return 0.5 * value * (1.0 + jnp.tanh(inner))


def mlp_kernel(steps, parts, has_base, *refs):
    rows_refs, refs = refs[:parts], refs[parts:]
    w_in_refs, w_out_refs, refs = refs[0:2], refs[2:4], refs[4:]
    base_refs = refs[:parts] if has_base else None
    out_refs, acc_refs = refs[-2 * parts : -parts], refs[-parts:]
    j = pl.program_id(0)

    @pl.when(j == 0)
    def _():
        for p in range(parts):
            if has_base:
                acc_refs[p][...] = base_refs[p][...].astype(jnp.float32)
            else:
                acc_refs[p][...] = jnp.zeros_like(acc_refs[p])

    for block in range(2):

        @pl.when(j // steps == block)
        def _():
            for p in range(parts):
                up = jnp.dot(
                    rows_refs[p][...], w_in_refs[block][...], preferred_element_type=jnp.float32
                )
                hidden = gelu(up).astype(jnp.bfloat16)
                acc_refs[p][...] += jnp.dot(
                    hidden, w_out_refs[block][...], preferred_element_type=jnp.float32
                )

    @pl.when(j == 2 * steps - 1)
    def _():
        for p in range(parts):
            out_refs[p][...] = acc_refs[p][...].astype(out_refs[p].dtype)


def mlp(rows, w_ins, w_outs, base, out_dtype, most=512):
    parts = len(rows)
    count, width = rows[0].shape
    units = w_ins[0].shape[1]
    tile = most if units % most == 0 else units
    steps = units // tile

    def in_map(block):
        return lambda j: (0, jnp.clip(j - block * steps, 0, steps - 1))

    def out_map(block):
        return lambda j: (jnp.clip(j - block * steps, 0, steps - 1), 0)

    whole = pl.BlockSpec((count, width), lambda j: (0, 0))
    in_specs = [whole] * parts
    in_specs += [pl.BlockSpec((width, tile), in_map(b)) for b in range(2)]
    in_specs += [pl.BlockSpec((tile, width), out_map(b)) for b in range(2)]
    operands = [*rows, *w_ins, *w_outs]
    if base is not None:
        in_specs += [whole] * parts
        operands += [*base]
    return pl.pallas_call(
        functools.partial(mlp_kernel, steps, parts, base is not None),
        grid=(2 * steps,),
        out_shape=[jax.ShapeDtypeStruct((count, width), out_dtype)] * parts,
        in_specs=in_specs,
        out_specs=[whole] * parts,
        scratch_shapes=[pltpu.VMEM((count, width), jnp.float32)] * parts,
        compiler_params=pltpu.CompilerParams(
            vmem_limit_bytes=60 * MIB, dimension_semantics=("arbitrary",)
        ),
        cost_estimate=pl.CostEstimate(
            flops=8 * parts * count * width * units,
            bytes_accessed=8 * width * units + 10 * parts * count * width,
            transcendentals=2 * parts * count * units,
        ),
    )(*operands)


def attention_kernel(key_tile, q_ref, k_ref, v_ref, out_ref):
    queries = q_ref[...]
    factor = math.log2(math.e) / math.sqrt(HD)
    width = queries.shape[1]
    total = jnp.zeros((1, width), jnp.float32)
    summed = jnp.zeros((HD, width), jnp.float32)
    for start in range(0, k_ref.shape[0], key_tile):
        part = pl.ds(start, key_tile)
        scores = jnp.dot(k_ref[part, :], queries, preferred_element_type=jnp.float32)
        weights = jnp.exp2(scores * factor)
        total += jnp.sum(weights, axis=0, keepdims=True)
        summed += jnp.dot(
            v_ref[:, part], weights.astype(jnp.bfloat16), preferred_element_type=jnp.float32
        )
    out_ref[...] = (summed / total).astype(out_ref.dtype)


def attention(queries, keys, values):
    columns = queries.shape[1]
    key_count = keys.shape[0]
    tile = 512 if columns % 512 == 0 else columns
    key_tile = 512 if key_count % 512 == 0 else key_count
    return pl.pallas_call(
        functools.partial(attention_kernel, key_tile),
        grid=(columns // tile,),
        out_shape=jax.ShapeDtypeStruct((HD, columns), jnp.bfloat16),
        in_specs=[
            pl.BlockSpec((HD, tile), lambda j: (0, j)),
            pl.BlockSpec((key_count, HD), lambda j: (0, 0)),
            pl.BlockSpec((HD, key_count), lambda j: (0, 0)),
        ],
        out_specs=pl.BlockSpec((HD, tile), lambda j: (0, j)),
        compiler_params=pltpu.CompilerParams(
            vmem_limit_bytes=48 * MIB, dimension_semantics=("arbitrary",)
        ),
        cost_estimate=pl.CostEstimate(
            flops=4 * HD * columns * key_count,
            bytes_accessed=4 * HD * (columns + key_count),
            transcendentals=columns * key_count,
        ),
    )(queries, keys, values)


def shards(places, tokens, router_w, expert_ids, w_in, w_out, w_qkv):
    row_count = tokens.shape[1]
    width = tokens.shape[2]
    experts = router_w.shape[1]
    slots = max(2, 3 * row_count // experts)
    columns = [[e * SPLIT + q for e in range(experts)] for q in range(SPLIT)]

    def across(value, bit):
        return lax.ppermute(value, "expert", [(p, p ^ bit) for p in range(places)])

    def other_core(value):
        return lax.ppermute(value, "seq", [(0, 1), (1, 0)])

    own_weights = (w_in[0], w_out[0])
    far_weights = tuple(across(w, 1) for w in own_weights)
    core_weights = tuple(other_core(w) for w in own_weights)

    own_tokens = tokens[0]
    own_ids = expert_ids[0]
    normed = layer_norm(own_tokens)
    logits = jnp.dot(normed, router_w, preferred_element_type=jnp.float32)
    expert_range = jnp.arange(experts, dtype=jnp.int32)
    first_pick = jnp.sum(jnp.where(own_ids[:, 0:1] == expert_range[None, :], logits, 0.0), axis=1)
    second_pick = jnp.sum(jnp.where(own_ids[:, 1:2] == expert_range[None, :], logits, 0.0), axis=1)
    first_gate = jax.nn.sigmoid(first_pick - second_pick)
    second_gate = jax.nn.sigmoid(second_pick - first_pick)
    pair_ids = own_ids.reshape(row_count * 2)
    onehot = (pair_ids[:, None] == expert_range[None, :]).astype(jnp.int32)
    before = jnp.cumsum(onehot, axis=0) - onehot
    position = jnp.sum(before * onehot, axis=1)
    slot_index = jnp.where(position < slots, pair_ids * slots + position, -1)
    slot_index = slot_index.reshape(row_count, 2)
    parts = 2 if slots % 2 == 0 else 1
    part_slots = slots // parts
    slot_range = (
        jnp.arange(experts, dtype=jnp.int32)[:, None] * slots
        + jnp.arange(part_slots, dtype=jnp.int32)[None, :]
    ).reshape(1, experts * part_slots)

    def between_planes(value):
        return lax.all_to_all(
            value.reshape(experts, -1, width),
            "expert",
            split_axis=0,
            concat_axis=0,
            tiled=True,
            axis_index_groups=columns,
        )

    packed, gate_parts = [], []
    for p in range(parts):
        is_first = slot_index[:, 0:1] == slot_range + p * part_slots
        is_second = slot_index[:, 1:2] == slot_range + p * part_slots
        select = (is_first | is_second).astype(jnp.bfloat16)
        rows = lax.dot_general(
            select, normed, (((0,), (0,)), ((), ())), preferred_element_type=jnp.float32
        ).astype(jnp.bfloat16)
        packed.append(rows.reshape(experts, part_slots, width))
        gates = jnp.where(is_first, first_gate[:, None], 0.0) + jnp.where(
            is_second, second_gate[:, None], 0.0
        )
        high = gates.astype(jnp.bfloat16)
        gate_parts.append((high, (gates - high.astype(jnp.float32)).astype(jnp.bfloat16)))

    received = between_planes(jnp.concatenate(packed, axis=1))
    near_rows = [
        received[:, p * part_slots : (p + 1) * part_slots].reshape(experts * part_slots, width)
        for p in range(parts)
    ]
    far_rows = [across(value, 2) for value in near_rows]
    chip_in, chip_out = zip(own_weights, core_weights)
    near_sum = mlp(near_rows, chip_in, chip_out, None, jnp.float32)
    far_sum = mlp(far_rows, chip_in, chip_out, None, jnp.float32)
    far_in, near_sum, far_sum = lax.optimization_barrier((far_weights[0], near_sum, far_sum))
    far_core_in = other_core(far_in)
    far_out, far_core_in, far_sum = lax.optimization_barrier(
        (far_weights[1], far_core_in, far_sum)
    )
    far_weights = (far_in, far_out)
    far_core_weights = (far_core_in, other_core(far_out))
    next_in, next_out = zip(far_weights, far_core_weights)
    sent = []
    for p in range(parts):
        sent += mlp(far_rows[p : p + 1], next_in, next_out, far_sum[p : p + 1], jnp.bfloat16)
        if p + 1 < parts:
            sent[p], far_sum = lax.optimization_barrier((sent[p], far_sum))
    arrived = [across(value, 2) for value in sent]
    near_sum, sent[-1] = lax.optimization_barrier((near_sum, sent[-1]))
    near_sum = [
        mlp(near_rows[p : p + 1], next_in, next_out, near_sum[p : p + 1], jnp.float32)[0]
        for p in range(parts)
    ]
    combined = own_tokens.astype(jnp.float32)
    for p in range(parts):
        summed = (near_sum[p] + arrived[p].astype(jnp.float32)).astype(jnp.bfloat16)
        merged = between_planes(summed).reshape(experts * part_slots, width)
        for gate in gate_parts[p]:
            combined += jnp.dot(gate, merged, preferred_element_type=jnp.float32)
    mixed = combined.astype(jnp.bfloat16)
    attn_local = layer_norm(mixed)
    attn_other = other_core(attn_local)
    own_proj, other_proj = [
        jnp.einsum("cdf,rd->cfr", w_qkv, value, preferred_element_type=jnp.float32).astype(
            jnp.bfloat16
        )
        for value in (attn_local, attn_other)
    ]
    images = 2
    is_low = lax.axis_index("seq") == 0
    proj = jnp.stack(
        [jnp.where(is_low, own_proj, other_proj), jnp.where(is_low, other_proj, own_proj)], axis=1
    )
    heads = proj.shape[2] // HD
    pairs = images * heads
    share = places // pairs
    part = row_count // share
    proj = proj.reshape(3, pairs, HD, row_count)
    query_parts = proj[0].reshape(pairs, HD, share, part).transpose(0, 2, 1, 3)
    key_parts = jnp.broadcast_to(proj[1][:, None], (pairs, share, HD, row_count))
    value_parts = jnp.broadcast_to(proj[2][:, None], (pairs, share, HD, row_count))
    leaving = jnp.concatenate([key_parts, value_parts, query_parts], axis=3).reshape(
        places, HD, 2 * row_count + part
    )
    landed = lax.all_to_all(leaving, "expert", split_axis=0, concat_axis=0, tiled=True)
    keys = landed[:, :, :row_count].transpose(0, 2, 1).reshape(places * row_count, HD)
    values = landed[:, :, row_count : 2 * row_count].transpose(1, 0, 2)
    values = values.reshape(HD, places * row_count)
    queries = landed[:, :, 2 * row_count :].transpose(1, 0, 2).reshape(HD, places * part)
    result = attention(queries, keys, values)
    result = result.reshape(HD, places, part).transpose(1, 0, 2)
    returned = lax.all_to_all(result, "expert", split_axis=0, concat_axis=0, tiled=True)
    attended = returned.reshape(images, heads, share, HD, part).transpose(0, 2, 4, 1, 3)
    attended = attended.reshape(images, row_count, heads * HD)
    return (mixed[None], attended)


def solution(mesh):
    in_specs = (
        P(("group", "seq"), "expert", None),
        P(),
        P(("group", "seq"), "expert", None),
        P("expert", None, "seq"),
        P("expert", "seq", None),
        P(None, None, "seq"),
    )
    out_specs = (P(("group", "seq"), "expert", None), P("group", "expert", "seq"))
    return jax.shard_map(
        functools.partial(shards, mesh.shape["expert"]),
        mesh=mesh,
        in_specs=in_specs,
        out_specs=out_specs,
        check_vma=False,
    )
```
